32 devices in a mesh: ctx: 16 (over z, x, core), head: 2 (over y).
Axes of the slice: x: 2, y: 2, z: 4, core: 2. Of those that a mesh axis runs over, the one named last changes fastest.
Arguments:
- query_rows: bfloat16 [16384, 1024], P('ctx', 'head'), may hold values from -8 to 8
- key_rows: bfloat16 [16384, 1024], P('ctx', 'head'), may hold values from -8 to 8
- value_rows: bfloat16 [16384, 1024], P('ctx', 'head'), may hold values from -6 to 6
- out_grad: bfloat16 [16384, 1024], P('ctx', 'head'), may hold values from -6 to 6
- out_weight: bfloat16 [1024, 1024], P('head'), may hold values from -0.1875 to 0.1875
- neighbours: int32 [128, 12], replicated, may hold values from 0 to 127, as said below
- counts: int32 [128], replicated, may hold values from 3 to 12, as said below
Outputs:
- query_grad: bfloat16 [16384, 1024], P('ctx', 'head')
- key_grad: bfloat16 [16384, 1024], P('ctx', 'head')
- value_grad: bfloat16 [16384, 1024], P('ctx', 'head')
- weight_grad: float32 [1024, 1024], P('head')
The draws below stay inside these ranges and needn't reach their ends.
Inputs may be any that keep to these rules, and one draw needn't show every extreme that they name: `neighbours`: row g names block g in slot 0, then distinct blocks held by ctx indices g // 8 - 1 to g // 8 + 1; slots 1 and 2 include a block of each of the ctx indices g // 8 - 1 and g // 8 + 1 that exists; slots from counts[g] on hold g again. `counts`: block 0 uses all 12 slots.
All inputs are finite; a program needn't handle non-finite values.
Results may differ from the reference program's by a relative error of at most 0.012.
The reference program's roundings to bfloat16 on the way (of `soft_weights`, `attended`, `grad_attended` and `grad_scores`) count: a program that leaves them out, or rounds other values in their place, can miss the bound.
Values may be sent and summed in bfloat16 or wider, within the bound.
A program may use at most 128 MiB of HBM per device.

```python
import jax
import jax.numpy as jnp
from jax import lax

H = 16
HD = 64
D = 1024
BS = 128
MAXNB = 12
NBD = 8
NBLK = 128
NODES = 16384


def draw_attention_pair(key):
    key = jax.random.fold_in(key, 29)
    queries = jnp.clip(jax.random.normal(jax.random.fold_in(key, 1), (NODES, D), jnp.float32), -6.0, 6.0)
    keys_drawn = jnp.clip(jax.random.normal(jax.random.fold_in(key, 2), (NODES, D), jnp.float32), -6.0, 6.0)
    return (queries, keys_drawn)


def draw_query_rows(key, part):
    return draw_attention_pair(key)[0].astype(jnp.bfloat16)


def draw_key_rows(key, part):
    return draw_attention_pair(key)[1].astype(jnp.bfloat16)


def draw_graph(key):
    key = jax.random.fold_in(key, 17)
    block_ids = jnp.arange(NBLK, dtype=jnp.int32)
    holder = block_ids // NBD
    least = min(3, MAXNB)
    levels = jax.random.randint(jax.random.fold_in(key, 1), (NBLK // NBD,), 0, 4)
    spread = jnp.maximum(1, (MAXNB - least + 1) * (levels + 1) // 4)[holder]
    counts = least + jax.random.randint(jax.random.fold_in(key, 2), (NBLK,), 0, 1 << 20) % spread
    counts = jnp.minimum(counts, MAXNB)
    counts = counts.at[0].set(MAXNB)
    places = jnp.arange(3 * NBD, dtype=jnp.int32)
    candidates = (holder[:, None] - 1) * NBD + places[None, :]
    usable = (candidates >= 0) & (candidates < NBLK) & (candidates != block_ids[:, None])
    jitter = jax.random.randint(jax.random.fold_in(key, 3), (NBLK, 3 * NBD), 0, 2 ** 14)
    lower_group = places < NBD
    upper_group = places >= 2 * NBD
    group_key = jitter * 256 + places[None, :]
    lower_best = jnp.argmin(jnp.where(lower_group[None, :], group_key, 2 ** 30), axis=1)
    upper_best = jnp.argmin(jnp.where(upper_group[None, :], group_key, 2 ** 30), axis=1)
    first_tier = (places[None, :] == lower_best[:, None]) | (places[None, :] == upper_best[:, None])
    tier = jnp.where(usable, jnp.where(first_tier, 0, 1), 2)
    ranking = tier * 2 ** 23 + group_key
    ranked = jnp.argsort(ranking, axis=1, stable=True)[:, :MAXNB - 1]
    picked = jnp.take_along_axis(candidates, ranked, axis=1)
    listed = jnp.concatenate([block_ids[:, None], picked], axis=1)
    slot_ids = jnp.arange(MAXNB, dtype=jnp.int32)
    listed = jnp.where(slot_ids[None, :] < counts[:, None], listed, block_ids[:, None])
    return (listed.astype(jnp.int32), counts.astype(jnp.int32))


def draw_neighbours(key, part):
    return draw_graph(key)[0]


def draw_counts(key, part):
    return draw_graph(key)[1]


def block_scale(key, extent, cuts, low, largest):
    factor_of, own = 1.0, jax.random.fold_in(key, 6)
    for axis_at, parts in cuts:
        draws = jnp.exp(jax.random.uniform(jax.random.fold_in(own, axis_at), (parts,), jnp.float32, low / len(cuts), largest / len(cuts)))
        factor_of = factor_of * jnp.repeat(draws, extent[axis_at] // parts).reshape([-1 if axis == axis_at else 1 for axis in range(len(extent))])
    return factor_of


def gaussian(own_key, extent, scale, reach, split=(), kind=jnp.bfloat16):
    loudness = block_scale(own_key, extent, split, -0.22, 0.18) if split else 1.0
    values = jax.random.normal(own_key, extent, jnp.float32) * scale * loudness
    return jnp.minimum(jnp.maximum(values, -reach), reach).astype(kind)


def setup_inputs(seed: int = 0) -> dict:
    key_of = jax.random.split(jax.random.key(seed), 8)
    return {
        "query_rows": draw_query_rows(jax.random.fold_in(key_of[7], 71), 0),
        "key_rows": draw_key_rows(jax.random.fold_in(key_of[7], 71), 0),
        "value_rows": gaussian(key_of[2], (NODES, D), 1.0, 6.0, ((0, 16), (1, 2))),
        "out_grad": gaussian(key_of[3], (NODES, D), 1.0, 6.0, ((0, 16), (1, 2))),
        "out_weight": gaussian(key_of[4], (D, D), D ** -0.5, 0.1875, ((0, 2),)),
        "neighbours": draw_neighbours(jax.random.fold_in(key_of[7], 71), 0),
        "counts": draw_counts(jax.random.fold_in(key_of[7], 71), 0),
    }


def to_bf16_kept(values):
    return lax.optimization_barrier(values.astype(jnp.bfloat16)).astype(jnp.float32)


def reference(query_rows, key_rows, value_rows, out_grad, out_weight, neighbours, counts):
    factor = HD ** -0.5
    query_blocks = query_rows.reshape(NBLK, BS, H, HD).astype(jnp.float32)
    key_blocks = key_rows.reshape(NBLK, BS, H, HD).astype(jnp.float32)
    value_blocks = value_rows.reshape(NBLK, BS, H, HD).astype(jnp.float32)
    slot_ids = jnp.arange(MAXNB, dtype=jnp.int32)

    def gather_keys(block_index):
        listed = neighbours[block_index]
        usable = slot_ids < counts[block_index]
        key_mask = jnp.repeat(usable, BS)
        picked_keys = key_blocks[listed].reshape(MAXNB * BS, H, HD)
        picked_values = value_blocks[listed].reshape(MAXNB * BS, H, HD)
        return listed, key_mask, picked_keys, picked_values

    def masked_scores(query_block, picked_keys, key_mask):
        scores = jnp.einsum("qhd,khd->hqk", query_block, picked_keys) * factor
        return jnp.where(key_mask[None, None, :], scores, -1e30)

    def forward_block(block_index):
        listed, key_mask, picked_keys, picked_values = gather_keys(block_index)
        scores = masked_scores(query_blocks[block_index], picked_keys, key_mask)
        highest = jnp.max(scores, axis=2)
        log_total = highest + jnp.log(jnp.sum(jnp.exp(scores - highest[:, :, None]), axis=2))
        soft_weights = to_bf16_kept(jnp.exp(scores - log_total[:, :, None]))
        attended = jnp.einsum("hqk,khd->qhd", soft_weights, picked_values)
        return attended.astype(jnp.bfloat16), log_total

    attended_blocks, log_totals = lax.map(forward_block, jnp.arange(NBLK, dtype=jnp.int32))
    attended = attended_blocks.reshape(NODES, D)
    grad_attended = jnp.dot(out_grad, out_weight.T, preferred_element_type=jnp.float32).astype(jnp.bfloat16)
    weight_grad = jnp.dot(attended.T, out_grad, preferred_element_type=jnp.float32) * (NODES ** -0.5)
    grad_blocks = grad_attended.reshape(NBLK, BS, H, HD).astype(jnp.float32)
    row_dots = jnp.sum(grad_blocks * attended_blocks.astype(jnp.float32), axis=3)

    def backward_block(totals, block_index):
        key_total, value_total = totals
        listed, key_mask, picked_keys, picked_values = gather_keys(block_index)
        query_block = query_blocks[block_index]
        grad_block = grad_blocks[block_index]
        scores = masked_scores(query_block, picked_keys, key_mask)
        soft_full = jnp.exp(scores - log_totals[block_index][:, :, None])
        grad_weights = jnp.einsum("qhd,khd->hqk", grad_block, picked_values)
        grad_scores = to_bf16_kept(soft_full * (grad_weights - row_dots[block_index].T[:, :, None]))
        soft_weights = to_bf16_kept(soft_full)
        grad_query = jnp.einsum("hqk,khd->qhd", grad_scores, picked_keys) * factor
        grad_key = jnp.einsum("hqk,qhd->khd", grad_scores, query_block) * factor
        grad_value = jnp.einsum("hqk,qhd->khd", soft_weights, grad_block)
        key_total = key_total.at[listed].add(grad_key.reshape(MAXNB, BS, D))
        value_total = value_total.at[listed].add(grad_value.reshape(MAXNB, BS, D))
        return (key_total, value_total), grad_query.astype(jnp.bfloat16)

    blank_totals = jnp.zeros((NBLK, BS, D), jnp.float32)
    (key_total, value_total), grad_queries = lax.scan(backward_block, (blank_totals, blank_totals), jnp.arange(NBLK, dtype=jnp.int32))
    query_grad = grad_queries.reshape(NODES, D)
    key_grad = key_total.reshape(NODES, D).astype(jnp.bfloat16)
    value_grad = value_total.reshape(NODES, D).astype(jnp.bfloat16)
    return (query_grad, key_grad, value_grad, weight_grad)
```

```python
import functools

import jax
import jax.numpy as jnp
from jax import lax
from jax.experimental import pallas as pl
from jax.experimental.pallas import tpu as pltpu
from jax.sharding import PartitionSpec as P

HD = 64
BS = 128
LANES = 2 * HD
STEP = 2
FACTOR = HD ** (-0.5)

NN = (((1,), (0,)), ((), ()))
NT = (((1,), (1,)), ((), ()))


def mm(a, b, dims):
    return lax.dot_general(a, b, dims, preferred_element_type=jnp.float32)


def shifted(x, axis, by):
    count = lax.axis_size(axis)
    pairs = [(i, i + by) for i in range(count) if 0 <= i + by < count]
    return lax.ppermute(x, axis, pairs)


def stacked(rows):
    lane = lax.broadcasted_iota(jnp.int32, rows.shape, 1)
    first = jnp.where(lane < HD, rows, 0.0)
    second = jnp.where(lane >= HD, rows, 0.0)
    return jnp.concatenate([first, second], axis=0).astype(jnp.bfloat16)


def own_parts(both):
    return jnp.concatenate([both[:HD, :BS], both[HD:, BS:]], axis=0)


def fold(values, op):
    return op(values.reshape(values.shape[0] // 8, 8, values.shape[1]), axis=0)


def attention_kernel(
    places,
    active,
    q_ref,
    g_ref,
    k_mid,
    v_mid,
    left_ref,
    right_ref,
    att_ref,
    dq_ref,
    out_left,
    out_mid,
    out_right,
    kw,
    vw,
    kt,
    vt,
    sc,
    dk,
    dv,
    *,
    blocks,
    slots,
    pairs,
):
    block = pl.program_id(0)
    width = pairs * LANES

    @pl.when(block == 0)
    def _():
        dk[...] = jnp.zeros_like(dk)
        dv[...] = jnp.zeros_like(dv)

        def place_block(b, carry):
            rows = pl.ds(pl.multiple_of(b * BS, BS), BS)
            for p in range(pairs):
                cols = slice(p * LANES, (p + 1) * LANES)
                vcols = slice(width + p * LANES, width + (p + 1) * LANES)
                for part, (kr, kc, vr, vc) in enumerate(
                    (
                        (left_ref, cols, left_ref, vcols),
                        (k_mid, cols, v_mid, cols),
                        (right_ref, cols, right_ref, vcols),
                    )
                ):
                    at = part * blocks + b
                    kb = kr[rows, kc]
                    vb = vr[rows, vc]
                    kw[p, at] = kb
                    vw[p, at] = vb
                    kt[p, at] = kb.T
                    vt[p, at] = vb.T
            return carry

        lax.fori_loop(0, blocks, place_block, 0)

    count = active[block]
    trips = (count + STEP - 1) // STEP
    base = block * slots
    chunk = STEP * BS

    q2, g2, gt = [], [], []
    for p in range(pairs):
        cols = slice(p * LANES, (p + 1) * LANES)
        q2.append(stacked(q_ref[:, cols].astype(jnp.float32)))
        g = g_ref[:, cols].astype(jnp.float32)
        g2.append(stacked(g))
        gt.append(g.T)
    qs = [(q * FACTOR).astype(jnp.bfloat16) for q in q2]

    def slot_places(t):
        return [places[base + t * STEP + u] for u in range(STEP)]

    def score_step(t, highest):
        at = slot_places(t)
        highest = list(highest)
        for u in range(STEP):
            used = t * STEP + u < count
            rows = pl.ds(pl.multiple_of(t * chunk + u * BS, BS), BS)
            for p in range(pairs):
                s = mm(kw[p, at[u]], qs[p], NT)
                s = jnp.where(used, s, -1e30)
                sc[p, rows, :] = s
                highest[p] = jnp.maximum(highest[p], fold(s, jnp.max))
        return tuple(highest)

    lowest = jnp.full((8, 2 * BS), -1e30, jnp.float32)
    highest = lax.fori_loop(0, trips, score_step, (lowest,) * pairs)
    highest = [jnp.max(x, axis=0, keepdims=True) for x in highest]

    def exp_step(t, total):
        rows = pl.ds(pl.multiple_of(t * chunk, chunk), chunk)
        total = list(total)
        for p in range(pairs):
            e = jnp.exp(sc[p, rows, :] - highest[p])
            sc[p, rows, :] = e
            total[p] = total[p] + fold(e, jnp.sum)
        return tuple(total)

    total = lax.fori_loop(0, trips, exp_step, (jnp.zeros((8, 2 * BS), jnp.float32),) * pairs)
    inverse = [1.0 / jnp.sum(x, axis=0, keepdims=True) for x in total]

    def sum_step(t, acc):
        at = slot_places(t)
        rows = pl.ds(pl.multiple_of(t * chunk, chunk), chunk)
        acc = list(acc)
        for p in range(pairs):
            w = (sc[p, rows, :] * inverse[p]).astype(jnp.bfloat16)
            v_t = jnp.concatenate([vt[p, a] for a in at], axis=1)
            acc[p] = acc[p] + mm(v_t, w, NN)
        return tuple(acc)

    blank = jnp.zeros((LANES, 2 * BS), jnp.float32)
    acc = lax.fori_loop(0, trips, sum_step, (blank,) * pairs)
    dots = []
    for p in range(pairs):
        cols = slice(p * LANES, (p + 1) * LANES)
        o_t = own_parts(acc[p]).astype(jnp.bfloat16).astype(jnp.float32)
        att_ref[:, cols] = o_t.T.astype(jnp.bfloat16)
        prod = o_t * gt[p]
        dots.append(
            jnp.concatenate(
                [
                    jnp.sum(prod[:HD], axis=0, keepdims=True),
                    jnp.sum(prod[HD:], axis=0, keepdims=True),
                ],
                axis=1,
            )
        )

    def grad_step(t, acc):
        at = slot_places(t)
        acc = list(acc)
        for p in range(pairs):
            ds_all = []
            for u in range(STEP):
                rows = pl.ds(pl.multiple_of(t * chunk + u * BS, BS), BS)
                w = sc[p, rows, :] * inverse[p]
                dp = mm(vw[p, at[u]], g2[p], NT)
                ds = (w * (dp - dots[p])).astype(jnp.bfloat16)
                dv[p, at[u]] += mm(w.astype(jnp.bfloat16), g2[p], NN)
                dk[p, at[u]] += mm(ds, q2[p], NN)
                ds_all.append(ds)
            k_t = jnp.concatenate([kt[p, a] for a in at], axis=1)
            acc[p] = acc[p] + mm(k_t, jnp.concatenate(ds_all, axis=0), NN)
        return tuple(acc)

    acc = lax.fori_loop(0, trips, grad_step, (blank,) * pairs)
    for p in range(pairs):
        cols = slice(p * LANES, (p + 1) * LANES)
        dq_ref[:, cols] = (own_parts(acc[p]).T * FACTOR).astype(jnp.bfloat16)

    @pl.when(block == blocks - 1)
    def _():
        def put_block(b, carry):
            rows = pl.ds(pl.multiple_of(b * BS, BS), BS)
            for p in range(pairs):
                cols = slice(p * LANES, (p + 1) * LANES)
                vcols = slice(width + p * LANES, width + (p + 1) * LANES)
                for part, out in enumerate((out_left, out_mid, out_right)):
                    at = part * blocks + b
                    out[rows, cols] = (dk[p, at] * FACTOR).astype(out.dtype)
                    out[rows, vcols] = dv[p, at].astype(out.dtype)
            return carry

        lax.fori_loop(0, blocks, put_block, 0)


def group_attention(places, active, queries, grads, keys, values, left, right, group, pairs):
    rows = queries.shape[0]
    blocks = rows // BS
    slots = places.shape[0] // blocks
    width = pairs * LANES
    tile = pl.BlockSpec((BS, width), lambda i, *_: (i, group))
    whole = pl.BlockSpec((rows, width), lambda i, *_: (0, group))
    out_tile = pl.BlockSpec((BS, width), lambda i, *_: (i, 0))
    packed = pl.BlockSpec((rows, 2 * width), lambda i, *_: (0, 0))
    window = (pairs, 3 * blocks, BS, LANES)
    padded = (slots + STEP - 1) // STEP * STEP
    return pl.pallas_call(
        functools.partial(attention_kernel, blocks=blocks, slots=slots, pairs=pairs),
        grid_spec=pltpu.PrefetchScalarGridSpec(
            num_scalar_prefetch=2,
            grid=(blocks,),
            in_specs=[tile, tile, whole, whole, packed, packed],
            out_specs=[out_tile, out_tile, packed, packed, packed],
            scratch_shapes=[
                pltpu.VMEM(window, jnp.bfloat16),
                pltpu.VMEM(window, jnp.bfloat16),
                pltpu.VMEM(window, jnp.bfloat16),
                pltpu.VMEM(window, jnp.bfloat16),
                pltpu.VMEM((pairs, padded * BS, 2 * BS), jnp.float32),
                pltpu.VMEM(window, jnp.float32),
                pltpu.VMEM(window, jnp.float32),
            ],
        ),
        out_shape=[
            jax.ShapeDtypeStruct((rows, width), jnp.bfloat16),
            jax.ShapeDtypeStruct((rows, width), jnp.bfloat16),
            jax.ShapeDtypeStruct((rows, 2 * width), jnp.bfloat16),
            jax.ShapeDtypeStruct((rows, 2 * width), jnp.float32),
            jax.ShapeDtypeStruct((rows, 2 * width), jnp.bfloat16),
        ],
        compiler_params=pltpu.CompilerParams(
            dimension_semantics=("arbitrary",), vmem_limit_bytes=48 * 1024 * 1024
        ),
        cost_estimate=pl.CostEstimate(
            flops=7 * 2 * 2 * blocks * slots * pairs * BS * BS * LANES,
            bytes_accessed=rows * width * 32,
            transcendentals=2 * blocks * slots * pairs * BS * BS,
        ),
    )(places, active, queries, grads, keys, values, left, right)


def body(query_rows, key_rows, value_rows, out_grad, out_weight, neighbours, counts):
    row_count, col_count = query_rows.shape
    blocks = row_count // BS
    slots = neighbours.shape[1]
    pair_total = col_count // LANES
    pairs = 2 if pair_total % 2 == 0 else 1
    groups = pair_total // pairs
    width = pairs * LANES
    ctx_index = lax.axis_index("ctx")
    head_index = lax.axis_index("head")

    halos = []
    for g in range(groups):
        cols = slice(g * width, (g + 1) * width)
        packed = jnp.concatenate([key_rows[:, cols], value_rows[:, cols]], axis=1)
        halos.append((shifted(packed, "ctx", 1), shifted(packed, "ctx", -1)))

    if lax.axis_size("head") == 2:
        other = lax.ppermute(out_grad, "head", [(0, 1), (1, 0)])
        first = jnp.where(head_index == 0, out_grad, other)
        second = jnp.where(head_index == 0, other, out_grad)
        cotangent = jnp.concatenate([first, second], axis=1)
    else:
        cotangent = lax.all_gather(out_grad, "head", axis=1, tiled=True)
    grad_attended = jnp.einsum(
        "ro,jo->rj", cotangent, out_weight, preferred_element_type=jnp.float32
    ).astype(jnp.bfloat16)

    first_block = ctx_index * blocks
    listed = lax.dynamic_slice_in_dim(neighbours, first_block, blocks, axis=0)
    active = lax.dynamic_slice_in_dim(counts, first_block, blocks, axis=0)
    places = jnp.clip(listed - (first_block - blocks), 0, 3 * blocks - 1)
    if slots % STEP:
        places = jnp.concatenate([places, places[:, :1]], axis=1)
    places = places.reshape(-1)
    scale = (row_count * lax.axis_size("ctx")) ** (-0.5)

    query_parts, key_parts, value_parts, weight_parts = [], [], [], []
    for g in range(groups):
        left, right = halos[g]
        attended, dq, to_left, middle, to_right = group_attention(
            places,
            active,
            query_rows,
            grad_attended,
            key_rows,
            value_rows,
            left,
            right,
            g,
            pairs,
        )
        product = jnp.einsum("rj,ro->jo", attended, cotangent, preferred_element_type=jnp.float32)
        weight_parts.append(lax.psum(product, "ctx") * scale)
        from_right = shifted(to_left, "ctx", -1).astype(jnp.float32)
        from_left = shifted(to_right, "ctx", 1).astype(jnp.float32)
        combined = (middle + from_right + from_left).astype(jnp.bfloat16)
        query_parts.append(dq)
        key_parts.append(combined[:, :width])
        value_parts.append(combined[:, width:])
    return (
        jnp.concatenate(query_parts, axis=1),
        jnp.concatenate(key_parts, axis=1),
        jnp.concatenate(value_parts, axis=1),
        jnp.concatenate(weight_parts, axis=0),
    )


def solution(mesh):
    placed = (
        P("ctx", "head"),
        P("ctx", "head"),
        P("ctx", "head"),
        P("ctx", "head"),
        P("head", None),
        P(),
        P(),
    )
    return jax.shard_map(
        body,
        mesh=mesh,
        in_specs=placed,
        out_specs=(P("ctx", "head"), P("ctx", "head"), P("ctx", "head"), P("head", None)),
        check_vma=False,
    )
```

```python
import functools

import jax
import jax.numpy as jnp
from jax import lax
from jax.experimental import pallas as pl
from jax.experimental.pallas import tpu as pltpu
from jax.sharding import PartitionSpec as P

HD = 64
BS = 128
LANES = 2 * HD
STEP = 2
FACTOR = HD ** (-0.5)

def mm(a, b):
    return jnp.dot(a, b, preferred_element_type=jnp.float32)


def shifted(x, axis, by):
    count = lax.axis_size(axis)
    pairs = [(i, i + by) for i in range(count) if 0 <= i + by < count]
    return lax.ppermute(x, axis, pairs)


def stacked(values, axis):
    at = lax.broadcasted_iota(jnp.int32, values.shape, axis)
    first = jnp.where(at < HD, values, 0.0)
    second = jnp.where(at >= HD, values, 0.0)
    return jnp.concatenate([first, second], axis=1 - axis).astype(jnp.bfloat16)


def own_parts(both):
    return jnp.concatenate([both[:HD, :BS], both[HD:, BS:]], axis=0)


def attention_kernel(
    places,
    active,
    q_ref,
    g_ref,
    k_mid,
    v_mid,
    left_ref,
    right_ref,
    att_ref,
    dq_ref,
    out_left,
    out_mid,
    out_right,
    kw,
    vw,
    kt,
    vt,
    fixed,
    fixed_t,
    sc,
    peak,
    mass,
    dk,
    dv,
    *,
    blocks,
    slots,
    pairs,
):
    block = pl.program_id(0)
    width = pairs * LANES

    @pl.when(block == 0)
    def _():
        dk[...] = jnp.zeros_like(dk)
        dv[...] = jnp.zeros_like(dv)

        def place_block(b, carry):
            rows = pl.ds(pl.multiple_of(b * BS, BS), BS)
            for p in range(pairs):
                cols = slice(p * LANES, (p + 1) * LANES)
                vcols = slice(width + p * LANES, width + (p + 1) * LANES)
                for part, (kr, kc, vr, vc) in enumerate(
                    (
                        (left_ref, cols, left_ref, vcols),
                        (k_mid, cols, v_mid, cols),
                        (right_ref, cols, right_ref, vcols),
                    )
                ):
                    at = part * blocks + b
                    kb = kr[rows, kc]
                    vb = vr[rows, vc]
                    kw[p, at] = kb
                    vw[p, at] = vb
                    kt[p, at] = kb.T
                    vt[p, at] = vb.T
            return carry

        lax.fori_loop(0, blocks, place_block, 0)

    count = active[block]
    trips = (count + STEP - 1) // STEP
    base = block * slots
    chunk = STEP * BS

    q_cols, g_cols, gt = [], [], []
    for p in range(pairs):
        cols = slice(p * LANES, (p + 1) * LANES)
        q = q_ref[:, cols].astype(jnp.float32)
        g = g_ref[:, cols].astype(jnp.float32)
        gt.append(g.T)
        fixed[p, 0] = stacked(q, 1)
        fixed[p, 1] = stacked(g, 1)
        q_cols.append(stacked(q.T * FACTOR, 0))
        g_cols.append(stacked(gt[p], 0))
    for p in range(pairs):
        fixed_t[p, 0] = q_cols[p]
        fixed_t[p, 1] = g_cols[p]

    def slot_places(t):
        return [places[base + t * STEP + u] for u in range(STEP)]

    for p in range(pairs):
        peak[p] = jnp.full(peak.shape[1:], -1e30, jnp.float32)
        mass[p] = jnp.zeros(mass.shape[1:], jnp.float32)

    def score_step(t, carry):
        at = slot_places(t)
        for p in range(pairs):
            both = mm(jnp.concatenate([kw[p, a] for a in at], axis=0), fixed_t[p, 0])
            for u in range(STEP):
                slot = t * STEP + u
                rows = pl.ds(pl.multiple_of(t * chunk + u * BS, BS), BS)
                s = both[u * BS : (u + 1) * BS]
                m = jnp.max(s, axis=0, keepdims=True)
                e = jnp.exp(s - m)
                sc[p, rows, :] = e
                peak[p, pl.ds(slot, 1), :] = jnp.where(slot < count, m, -1e30)
                mass[p, pl.ds(slot, 1), :] = jnp.sum(e, axis=0, keepdims=True)
        return carry

    lax.fori_loop(0, trips, score_step, 0)
    for p in range(pairs):
        ratio = jnp.exp(peak[p] - jnp.max(peak[p], axis=0, keepdims=True))
        total = jnp.sum(mass[p] * ratio, axis=0, keepdims=True)
        peak[p] = ratio * (1.0 / total)

    def weights(p, t, u):
        rows = pl.ds(pl.multiple_of(t * chunk + u * BS, BS), BS)
        return sc[p, rows, :] * peak[p, pl.ds(t * STEP + u, 1), :]

    def sum_step(t, acc):
        at = slot_places(t)
        acc = list(acc)
        for p in range(pairs):
            w = jnp.concatenate(
                [weights(p, t, u).astype(jnp.bfloat16) for u in range(STEP)], axis=0
            )
            v_t = jnp.concatenate([vt[p, a] for a in at], axis=1)
            acc[p] = acc[p] + mm(v_t, w)
        return tuple(acc)

    blank = jnp.zeros((LANES, 2 * BS), jnp.float32)
    acc = lax.fori_loop(0, trips, sum_step, (blank,) * pairs)
    dots = []
    for p in range(pairs):
        cols = slice(p * LANES, (p + 1) * LANES)
        o_t = own_parts(acc[p]).astype(jnp.bfloat16).astype(jnp.float32)
        att_ref[:, cols] = o_t.T.astype(jnp.bfloat16)
        prod = o_t * gt[p]
        dots.append(
            jnp.concatenate(
                [
                    jnp.sum(prod[:HD], axis=0, keepdims=True),
                    jnp.sum(prod[HD:], axis=0, keepdims=True),
                ],
                axis=1,
            )
        )

    def grad_step(t, acc):
        at = slot_places(t)
        acc = list(acc)
        for p in range(pairs):
            dp = mm(jnp.concatenate([vw[p, a] for a in at], axis=0), fixed_t[p, 1])
            w = [weights(p, t, u) for u in range(STEP)]
            ds = [w[u] * (dp[u * BS : (u + 1) * BS] - dots[p]) for u in range(STEP)]
            w = jnp.concatenate(w, axis=0).astype(jnp.bfloat16)
            ds = jnp.concatenate(ds, axis=0).astype(jnp.bfloat16)
            grad_v = mm(w, fixed[p, 1])
            grad_k = mm(ds, fixed[p, 0])
            k_t = jnp.concatenate([kt[p, a] for a in at], axis=1)
            acc[p] = acc[p] + mm(k_t, ds)
            for u in range(STEP):
                dv[p, at[u]] += grad_v[u * BS : (u + 1) * BS]
                dk[p, at[u]] += grad_k[u * BS : (u + 1) * BS]
        return tuple(acc)

    acc = lax.fori_loop(0, trips, grad_step, (blank,) * pairs)
    for p in range(pairs):
        cols = slice(p * LANES, (p + 1) * LANES)
        dq_ref[:, cols] = (own_parts(acc[p]).T * FACTOR).astype(jnp.bfloat16)

    @pl.when(block == blocks - 1)
    def _():
        def put_block(b, carry):
            rows = pl.ds(pl.multiple_of(b * BS, BS), BS)
            for p in range(pairs):
                cols = slice(p * LANES, (p + 1) * LANES)
                vcols = slice(width + p * LANES, width + (p + 1) * LANES)
                for part, out in enumerate((out_left, out_mid, out_right)):
                    at = part * blocks + b
                    out[rows, cols] = (dk[p, at] * FACTOR).astype(out.dtype)
                    out[rows, vcols] = dv[p, at].astype(out.dtype)
            return carry

        lax.fori_loop(0, blocks, put_block, 0)


def group_attention(places, active, queries, grads, keys, values, left, right, group, pairs):
    rows = queries.shape[0]
    blocks = rows // BS
    slots = places.shape[0] // blocks
    width = pairs * LANES
    tile = pl.BlockSpec((BS, width), lambda i, *_: (i, group))
    whole = pl.BlockSpec((rows, width), lambda i, *_: (0, group))
    out_tile = pl.BlockSpec((BS, width), lambda i, *_: (i, 0))
    packed = pl.BlockSpec((rows, 2 * width), lambda i, *_: (0, 0))
    window = (pairs, 3 * blocks, BS, LANES)
    padded = (slots + STEP - 1) // STEP * STEP
    return pl.pallas_call(
        functools.partial(attention_kernel, blocks=blocks, slots=slots, pairs=pairs),
        grid_spec=pltpu.PrefetchScalarGridSpec(
            num_scalar_prefetch=2,
            grid=(blocks,),
            in_specs=[tile, tile, whole, whole, packed, packed],
            out_specs=[out_tile, out_tile, packed, packed, packed],
            scratch_shapes=[
                pltpu.VMEM(window, jnp.bfloat16),
                pltpu.VMEM(window, jnp.bfloat16),
                pltpu.VMEM(window, jnp.bfloat16),
                pltpu.VMEM(window, jnp.bfloat16),
                pltpu.VMEM((pairs, 2, 2 * BS, LANES), jnp.bfloat16),
                pltpu.VMEM((pairs, 2, LANES, 2 * BS), jnp.bfloat16),
                pltpu.VMEM((pairs, padded * BS, 2 * BS), jnp.float32),
                pltpu.VMEM((pairs, (padded + 7) // 8 * 8, 2 * BS), jnp.float32),
                pltpu.VMEM((pairs, (padded + 7) // 8 * 8, 2 * BS), jnp.float32),
                pltpu.VMEM(window, jnp.float32),
                pltpu.VMEM(window, jnp.float32),
            ],
        ),
        out_shape=[
            jax.ShapeDtypeStruct((rows, width), jnp.bfloat16),
            jax.ShapeDtypeStruct((rows, width), jnp.bfloat16),
            jax.ShapeDtypeStruct((rows, 2 * width), jnp.bfloat16),
            jax.ShapeDtypeStruct((rows, 2 * width), jnp.float32),
            jax.ShapeDtypeStruct((rows, 2 * width), jnp.bfloat16),
        ],
        compiler_params=pltpu.CompilerParams(
            dimension_semantics=("arbitrary",), vmem_limit_bytes=48 * 1024 * 1024
        ),
        cost_estimate=pl.CostEstimate(
            flops=7 * 2 * 2 * blocks * slots * pairs * BS * BS * LANES,
            bytes_accessed=rows * width * 32,
            transcendentals=2 * blocks * slots * pairs * BS * BS,
        ),
    )(places, active, queries, grads, keys, values, left, right)


def sum_kernel(*refs, sizes, count):
    parts, (full, acc, send, *landing, send_sems, recv_sems) = refs[:count], refs[count:]
    me = lax.axis_index("ctx")
    stages = []
    stride = 1
    for size in sizes:
        stages.append((size, stride, lax.rem(me // stride, size)))
        stride *= size

    def peer(stage, away):
        size, stride, mine = stage
        other = lax.rem(mine + away, size)
        return other, me + (other - mine) * stride

    barrier = pltpu.get_barrier_semaphore()
    greeted = 0
    for stage in stages:
        for away in range(1, stage[0]):
            pl.semaphore_signal(
                barrier,
                inc=1,
                device_id={"ctx": peer(stage, away)[1]},
                device_id_type=pl.DeviceIdType.MESH,
            )
            greeted += 1
    at = 0
    for part in parts:
        acc[pl.ds(at, part.shape[0]), :] = part[...]
        at += part.shape[0]
    pl.semaphore_wait(barrier, greeted)

    def copy(src, dst, sem, device):
        return pltpu.make_async_remote_copy(
            src_ref=src,
            dst_ref=dst,
            send_sem=send_sems.at[sem],
            recv_sem=recv_sems.at[sem],
            device_id={"ctx": device},
            device_id_type=pl.DeviceIdType.MESH,
        )

    rows = acc.shape[0]
    start = 0
    sem = 0
    pending = []
    spans = []
    for stage, land in zip(stages, landing):
        size, _, mine = stage
        spans.append((start, rows))
        piece = rows // size
        copies = []
        for away in range(1, size):
            other, device = peer(stage, away)
            span = pl.ds(pl.multiple_of(start + other * piece, 16), piece)
            send[span, :] = acc[span, :].astype(jnp.bfloat16)
            one = copy(send.at[span, :], land.at[away - 1], sem, device)
            one.start()
            copies.append(one)
            sem += 1
        start = start + mine * piece
        own = pl.ds(pl.multiple_of(start, 16), piece)
        for one in copies:
            one.wait_recv()
        total = acc[own, :]
        for away in range(1, size):
            total = total + land[away - 1].astype(jnp.float32)
        acc[own, :] = total
        rows = piece
        pending += copies
    own = pl.ds(pl.multiple_of(start, 16), rows)
    full[own, :] = acc[own, :].astype(jnp.bfloat16)
    for stage, (outer, outer_rows) in zip(stages[::-1], spans[::-1]):
        size, _, mine = stage
        piece = outer_rows // size
        span = pl.ds(pl.multiple_of(outer + mine * piece, 16), piece)
        copies = []
        for away in range(1, size):
            one = copy(full.at[span, :], full.at[span, :], sem, peer(stage, away)[1])
            one.start()
            copies.append(one)
            sem += 1
        for one in copies:
            one.wait_recv()
        pending += copies
    for one in pending:
        one.wait_send()


def summed_over_ctx(parts):
    count = lax.axis_size("ctx")
    rows = sum(part.shape[0] for part in parts)
    cols = parts[0].shape[1]
    rest = count // 2
    inner = 2 if rest <= 8 else 8
    sizes = (2, inner, rest // inner)
    if rows % (16 * count) or 2 * inner * sizes[2] != count:
        return lax.psum(jnp.concatenate(parts, axis=0), "ctx")
    landing = []
    left = rows
    for size in sizes:
        left //= size
        landing.append(pltpu.VMEM((size - 1, left, cols), jnp.bfloat16))
    copies = 2 * sum(size - 1 for size in sizes)
    out = pl.pallas_call(
        functools.partial(sum_kernel, sizes=sizes, count=len(parts)),
        out_shape=jax.ShapeDtypeStruct((rows, cols), jnp.bfloat16),
        in_specs=[pl.BlockSpec(memory_space=pltpu.VMEM)] * len(parts),
        out_specs=pl.BlockSpec(memory_space=pltpu.VMEM),
        scratch_shapes=[
            pltpu.VMEM((rows, cols), jnp.float32),
            pltpu.VMEM((rows, cols), jnp.bfloat16),
            *landing,
            pltpu.SemaphoreType.DMA((copies,)),
            pltpu.SemaphoreType.DMA((copies,)),
        ],
        compiler_params=pltpu.CompilerParams(
            collective_id=0, has_side_effects=True, vmem_limit_bytes=32 * 1024 * 1024
        ),
        cost_estimate=pl.CostEstimate(
            flops=rows * cols * 4, bytes_accessed=rows * cols * 40, transcendentals=0
        ),
    )(*parts)
    return out.astype(jnp.float32)


def body(query_rows, key_rows, value_rows, out_grad, out_weight, neighbours, counts):
    row_count, col_count = query_rows.shape
    blocks = row_count // BS
    slots = neighbours.shape[1]
    pair_total = col_count // LANES
    pairs = 2 if pair_total % 2 == 0 else 1
    groups = pair_total // pairs
    width = pairs * LANES
    ctx_index = lax.axis_index("ctx")
    head_index = lax.axis_index("head")

    halos = []
    for g in range(groups):
        cols = slice(g * width, (g + 1) * width)
        packed = jnp.concatenate([key_rows[:, cols], value_rows[:, cols]], axis=1)
        halos.append((shifted(packed, "ctx", 1), shifted(packed, "ctx", -1)))

    if lax.axis_size("head") == 2:
        other = lax.ppermute(out_grad, "head", [(0, 1), (1, 0)])
        first = jnp.where(head_index == 0, out_grad, other)
        second = jnp.where(head_index == 0, other, out_grad)
        cotangent = jnp.concatenate([first, second], axis=1)
    else:
        cotangent = lax.all_gather(out_grad, "head", axis=1, tiled=True)
    grad_attended = jnp.einsum(
        "ro,jo->rj", cotangent, out_weight, preferred_element_type=jnp.float32
    ).astype(jnp.bfloat16)

    first_block = ctx_index * blocks
    listed = lax.dynamic_slice_in_dim(neighbours, first_block, blocks, axis=0)
    active = lax.dynamic_slice_in_dim(counts, first_block, blocks, axis=0)
    places = jnp.clip(listed - (first_block - blocks), 0, 3 * blocks - 1)
    if slots % STEP:
        places = jnp.concatenate([places, places[:, :1]], axis=1)
    places = places.reshape(-1)
    scale = (row_count * lax.axis_size("ctx")) ** (-0.5)

    query_parts, key_parts, value_parts, weight_parts = [], [], [], []
    for g in range(groups):
        left, right = halos[g]
        attended, dq, to_left, middle, to_right = group_attention(
            places,
            active,
            query_rows,
            grad_attended,
            key_rows,
            value_rows,
            left,
            right,
            g,
            pairs,
        )
        product = jnp.einsum("rj,ro->jo", attended, cotangent, preferred_element_type=jnp.float32)
        weight_parts.append(product)
        from_right = shifted(to_left, "ctx", -1).astype(jnp.float32)
        from_left = shifted(to_right, "ctx", 1).astype(jnp.float32)
        combined = (middle + from_right + from_left).astype(jnp.bfloat16)
        query_parts.append(dq)
        key_parts.append(combined[:, :width])
        value_parts.append(combined[:, width:])
    return (
        jnp.concatenate(query_parts, axis=1),
        jnp.concatenate(key_parts, axis=1),
        jnp.concatenate(value_parts, axis=1),
        summed_over_ctx(weight_parts) * scale,
    )


def solution(mesh):
    placed = (
        P("ctx", "head"),
        P("ctx", "head"),
        P("ctx", "head"),
        P("ctx", "head"),
        P("head", None),
        P(),
        P(),
    )
    return jax.shard_map(
        body,
        mesh=mesh,
        in_specs=placed,
        out_specs=(P("ctx", "head"), P("ctx", "head"), P("ctx", "head"), P("head", None)),
        check_vma=False,
    )
```

```python
import functools

import jax
import jax.numpy as jnp
from jax import lax
from jax.experimental import pallas as pl
from jax.experimental.pallas import tpu as pltpu
from jax.sharding import PartitionSpec as P

HD = 64
BS = 128
LANES = 2 * HD
STEPS = (4, 2)
FACTOR = HD ** (-0.5)

def mm(a, b):
    return jnp.dot(a, b, preferred_element_type=jnp.float32)


def shifted(x, axis, by):
    count = lax.axis_size(axis)
    pairs = [(i, i + by) for i in range(count) if 0 <= i + by < count]
    return lax.ppermute(x, axis, pairs)


def stacked(values, axis):
    at = lax.broadcasted_iota(jnp.int32, values.shape, axis)
    first = jnp.where(at < HD, values, 0.0)
    second = jnp.where(at >= HD, values, 0.0)
    return jnp.concatenate([first, second], axis=1 - axis).astype(jnp.bfloat16)


def own_parts(both):
    return jnp.concatenate([both[:HD, :BS], both[HD:, BS:]], axis=0)


def attention_kernel(
    places,
    active,
    *refs,
    blocks,
    slots,
    pairs,
):
    q_refs, g_refs, k_mids, v_mids = [refs[i * pairs : (i + 1) * pairs] for i in range(4)]
    (
        left_ref,
        right_ref,
        att_ref,
        dq_ref,
        out_left,
        out_mid,
        out_right,
        kw,
        vw,
        kt,
        vt,
        fixed,
        fixed_t,
        sc,
        peak,
        mass,
        acc,
        dk,
        dv,
    ) = refs[4 * pairs :]
    block = pl.program_id(0)
    width = pairs * LANES

    @pl.when(block == 0)
    def _():
        dk[...] = jnp.zeros_like(dk)
        dv[...] = jnp.zeros_like(dv)

        def place_block(b, carry):
            rows = pl.ds(pl.multiple_of(b * BS, BS), BS)
            for p in range(pairs):
                cols = slice(p * LANES, (p + 1) * LANES)
                vcols = slice(width + p * LANES, width + (p + 1) * LANES)
                for part, (kr, kc, vr, vc) in enumerate(
                    (
                        (left_ref, cols, left_ref, vcols),
                        (k_mids[p], slice(None), v_mids[p], slice(None)),
                        (right_ref, cols, right_ref, vcols),
                    )
                ):
                    at = part * blocks + b
                    kb = kr[rows, kc]
                    vb = vr[rows, vc]
                    kw[p, at] = kb
                    vw[p, at] = vb
                    kt[p, at] = kb.T
                    vt[p, at] = vb.T
            return carry

        lax.fori_loop(0, blocks, place_block, 0)

    count = active[block]
    large, small = STEPS
    full = (count + 1) // large
    rest = (jnp.maximum(count - full * large, 0) + small - 1) // small
    base = block * slots

    def sweep(visit):
        def large_trip(t, carry):
            visit(t * large, large)
            return carry

        def small_trip(t, carry):
            visit(full * large + t * small, small)
            return carry

        lax.fori_loop(0, full, large_trip, 0)
        lax.fori_loop(0, rest, small_trip, 0)

    q_cols, g_cols, gt = [], [], []
    for p in range(pairs):
        cols = slice(p * LANES, (p + 1) * LANES)
        q = q_refs[p][...].astype(jnp.float32)
        g = g_refs[p][...].astype(jnp.float32)
        gt.append(g.T)
        fixed[p, 0] = stacked(q, 1)
        fixed[p, 1] = stacked(g, 1)
        q_cols.append(stacked(q.T * FACTOR, 0))
        g_cols.append(stacked(gt[p], 0))
    for p in range(pairs):
        fixed_t[p, 0] = q_cols[p]
        fixed_t[p, 1] = g_cols[p]

    def slot_places(start, step):
        return [places[base + start + u] for u in range(step)]

    for p in range(pairs):
        peak[p] = jnp.full(peak.shape[1:], -1e30, jnp.float32)
        mass[p] = jnp.zeros(mass.shape[1:], jnp.float32)

    def score_step(start, step):
        at = slot_places(start, step)
        for p in range(pairs):
            both = mm(jnp.concatenate([kw[p, a] for a in at], axis=0), fixed_t[p, 0])
            for u in range(step):
                slot = start + u
                rows = pl.ds(pl.multiple_of(slot * BS, BS), BS)
                s = both[u * BS : (u + 1) * BS]
                m = jnp.max(s, axis=0, keepdims=True)
                e = jnp.exp(s - m)
                sc[p, rows, :] = e
                peak[p, pl.ds(slot, 1), :] = jnp.where(slot < count, m, -1e30)
                mass[p, pl.ds(slot, 1), :] = jnp.sum(e, axis=0, keepdims=True)

    sweep(score_step)
    for p in range(pairs):
        ratio = jnp.exp(peak[p] - jnp.max(peak[p], axis=0, keepdims=True))
        total = jnp.sum(mass[p] * ratio, axis=0, keepdims=True)
        peak[p] = ratio * (1.0 / total)

    def weights(p, slot):
        rows = pl.ds(pl.multiple_of(slot * BS, BS), BS)
        return sc[p, rows, :] * peak[p, pl.ds(slot, 1), :]

    def sum_step(start, step):
        at = slot_places(start, step)
        for p in range(pairs):
            w = jnp.concatenate(
                [weights(p, start + u).astype(jnp.bfloat16) for u in range(step)], axis=0
            )
            v_t = jnp.concatenate([vt[p, a] for a in at], axis=1)
            acc[p] += mm(v_t, w)

    acc[...] = jnp.zeros_like(acc)
    sweep(sum_step)
    dots = []
    for p in range(pairs):
        cols = slice(p * LANES, (p + 1) * LANES)
        o_t = own_parts(acc[p]).astype(jnp.bfloat16).astype(jnp.float32)
        att_ref[:, cols] = o_t.T.astype(jnp.bfloat16)
        prod = o_t * gt[p]
        dots.append(
            jnp.concatenate(
                [
                    jnp.sum(prod[:HD], axis=0, keepdims=True),
                    jnp.sum(prod[HD:], axis=0, keepdims=True),
                ],
                axis=1,
            )
        )

    def grad_step(start, step):
        at = slot_places(start, step)
        for p in range(pairs):
            dp = mm(jnp.concatenate([vw[p, a] for a in at], axis=0), fixed_t[p, 1])
            w = [weights(p, start + u) for u in range(step)]
            ds = [w[u] * (dp[u * BS : (u + 1) * BS] - dots[p]) for u in range(step)]
            w = jnp.concatenate(w, axis=0).astype(jnp.bfloat16)
            ds = jnp.concatenate(ds, axis=0).astype(jnp.bfloat16)
            grad_v = mm(w, fixed[p, 1])
            grad_k = mm(ds, fixed[p, 0])
            k_t = jnp.concatenate([kt[p, a] for a in at], axis=1)
            acc[p] += mm(k_t, ds)
            for u in range(step):
                dv[p, at[u]] += grad_v[u * BS : (u + 1) * BS]
                dk[p, at[u]] += grad_k[u * BS : (u + 1) * BS]

    acc[...] = jnp.zeros_like(acc)
    sweep(grad_step)
    for p in range(pairs):
        cols = slice(p * LANES, (p + 1) * LANES)
        dq_ref[:, cols] = (own_parts(acc[p]).T * FACTOR).astype(jnp.bfloat16)

    @pl.when(block == blocks - 1)
    def _():
        def put_block(b, carry):
            rows = pl.ds(pl.multiple_of(b * BS, BS), BS)
            for p in range(pairs):
                cols = slice(p * LANES, (p + 1) * LANES)
                vcols = slice(width + p * LANES, width + (p + 1) * LANES)
                for part, out in enumerate((out_left, out_mid, out_right)):
                    at = part * blocks + b
                    out[rows, cols] = (dk[p, at] * FACTOR).astype(out.dtype)
                    out[rows, vcols] = dv[p, at].astype(out.dtype)
            return carry

        lax.fori_loop(0, blocks, put_block, 0)


def group_attention(places, active, queries, grads, keys, values, left, right, start, pairs):
    rows = queries.shape[0]
    blocks = rows // BS
    slots = places.shape[0] // blocks
    width = pairs * LANES
    tiles = [pl.BlockSpec((BS, LANES), lambda i, *_, at=start + p: (i, at)) for p in range(pairs)]
    wholes = [pl.BlockSpec((rows, LANES), lambda i, *_, at=start + p: (0, at)) for p in range(pairs)]
    out_tile = pl.BlockSpec((BS, width), lambda i, *_: (i, 0))
    packed = pl.BlockSpec((rows, 2 * width), lambda i, *_: (0, 0))
    window = (pairs, 3 * blocks, BS, LANES)
    padded = slots
    return pl.pallas_call(
        functools.partial(attention_kernel, blocks=blocks, slots=slots, pairs=pairs),
        grid_spec=pltpu.PrefetchScalarGridSpec(
            num_scalar_prefetch=2,
            grid=(blocks,),
            in_specs=[*tiles, *tiles, *wholes, *wholes, packed, packed],
            out_specs=[out_tile, out_tile, packed, packed, packed],
            scratch_shapes=[
                pltpu.VMEM(window, jnp.bfloat16),
                pltpu.VMEM(window, jnp.bfloat16),
                pltpu.VMEM(window, jnp.bfloat16),
                pltpu.VMEM(window, jnp.bfloat16),
                pltpu.VMEM((pairs, 2, 2 * BS, LANES), jnp.bfloat16),
                pltpu.VMEM((pairs, 2, LANES, 2 * BS), jnp.bfloat16),
                pltpu.VMEM((pairs, padded * BS, 2 * BS), jnp.float32),
                pltpu.VMEM((pairs, (padded + 7) // 8 * 8, 2 * BS), jnp.float32),
                pltpu.VMEM((pairs, (padded + 7) // 8 * 8, 2 * BS), jnp.float32),
                pltpu.VMEM((pairs, LANES, 2 * BS), jnp.float32),
                pltpu.VMEM(window, jnp.float32),
                pltpu.VMEM(window, jnp.float32),
            ],
        ),
        out_shape=[
            jax.ShapeDtypeStruct((rows, width), jnp.bfloat16),
            jax.ShapeDtypeStruct((rows, width), jnp.bfloat16),
            jax.ShapeDtypeStruct((rows, 2 * width), jnp.bfloat16),
            jax.ShapeDtypeStruct((rows, 2 * width), jnp.float32),
            jax.ShapeDtypeStruct((rows, 2 * width), jnp.bfloat16),
        ],
        compiler_params=pltpu.CompilerParams(
            dimension_semantics=("arbitrary",), vmem_limit_bytes=48 * 1024 * 1024
        ),
        cost_estimate=pl.CostEstimate(
            flops=7 * 2 * 2 * blocks * slots * pairs * BS * BS * LANES,
            bytes_accessed=rows * width * 32,
            transcendentals=2 * blocks * slots * pairs * BS * BS,
        ),
    )(
        places,
        active,
        *[queries] * pairs,
        *[grads] * pairs,
        *[keys] * pairs,
        *[values] * pairs,
        left,
        right,
    )


def sum_kernel(*refs, sizes, count):
    parts, (full, acc, send, *landing, send_sems, recv_sems) = refs[:count], refs[count:]
    me = lax.axis_index("ctx")
    stages = []
    stride = 1
    for size in sizes:
        stages.append((size, stride, lax.rem(me // stride, size)))
        stride *= size

    def peer(stage, away):
        size, stride, mine = stage
        other = lax.rem(mine + away, size)
        return other, me + (other - mine) * stride

    barrier = pltpu.get_barrier_semaphore()
    greeted = 0
    for stage in stages:
        for away in range(1, stage[0]):
            pl.semaphore_signal(
                barrier,
                inc=1,
                device_id={"ctx": peer(stage, away)[1]},
                device_id_type=pl.DeviceIdType.MESH,
            )
            greeted += 1
    at = 0
    for part in parts:
        acc[pl.ds(at, part.shape[0]), :] = part[...]
        at += part.shape[0]
    pl.semaphore_wait(barrier, greeted)

    def copy(src, dst, sem, device):
        return pltpu.make_async_remote_copy(
            src_ref=src,
            dst_ref=dst,
            send_sem=send_sems.at[sem],
            recv_sem=recv_sems.at[sem],
            device_id={"ctx": device},
            device_id_type=pl.DeviceIdType.MESH,
        )

    rows = acc.shape[0]
    start = 0
    sem = 0
    pending = []
    spans = []
    for stage, land in zip(stages, landing):
        size, _, mine = stage
        spans.append((start, rows))
        piece = rows // size
        copies = []
        for away in range(1, size):
            other, device = peer(stage, away)
            span = pl.ds(pl.multiple_of(start + other * piece, 16), piece)
            send[span, :] = acc[span, :].astype(jnp.bfloat16)
            one = copy(send.at[span, :], land.at[away - 1], sem, device)
            one.start()
            copies.append(one)
            sem += 1
        start = start + mine * piece
        own = pl.ds(pl.multiple_of(start, 16), piece)
        for one in copies:
            one.wait_recv()
        total = acc[own, :]
        for away in range(1, size):
            total = total + land[away - 1].astype(jnp.float32)
        acc[own, :] = total
        rows = piece
        pending += copies
    own = pl.ds(pl.multiple_of(start, 16), rows)
    full[own, :] = acc[own, :].astype(jnp.bfloat16)
    for stage, (outer, outer_rows) in zip(stages[::-1], spans[::-1]):
        size, _, mine = stage
        piece = outer_rows // size
        span = pl.ds(pl.multiple_of(outer + mine * piece, 16), piece)
        copies = []
        for away in range(1, size):
            one = copy(full.at[span, :], full.at[span, :], sem, peer(stage, away)[1])
            one.start()
            copies.append(one)
            sem += 1
        for one in copies:
            one.wait_recv()
        pending += copies
    for one in pending:
        one.wait_send()


def summed_over_ctx(parts):
    count = lax.axis_size("ctx")
    rows = sum(part.shape[0] for part in parts)
    cols = parts[0].shape[1]
    rest = count // 2
    inner = 2 if rest <= 8 else 8
    sizes = (2, inner, rest // inner)
    if rows % (16 * count) or 2 * inner * sizes[2] != count:
        return lax.psum(jnp.concatenate(parts, axis=0), "ctx")
    landing = []
    left = rows
    for size in sizes:
        left //= size
        landing.append(pltpu.VMEM((size - 1, left, cols), jnp.bfloat16))
    copies = 2 * sum(size - 1 for size in sizes)
    out = pl.pallas_call(
        functools.partial(sum_kernel, sizes=sizes, count=len(parts)),
        out_shape=jax.ShapeDtypeStruct((rows, cols), jnp.bfloat16),
        in_specs=[pl.BlockSpec(memory_space=pltpu.VMEM)] * len(parts),
        out_specs=pl.BlockSpec(memory_space=pltpu.VMEM),
        scratch_shapes=[
            pltpu.VMEM((rows, cols), jnp.float32),
            pltpu.VMEM((rows, cols), jnp.bfloat16),
            *landing,
            pltpu.SemaphoreType.DMA((copies,)),
            pltpu.SemaphoreType.DMA((copies,)),
        ],
        compiler_params=pltpu.CompilerParams(
            collective_id=0, has_side_effects=True, vmem_limit_bytes=32 * 1024 * 1024
        ),
        cost_estimate=pl.CostEstimate(
            flops=rows * cols * 4, bytes_accessed=rows * cols * 40, transcendentals=0
        ),
    )(*parts)
    return out.astype(jnp.float32)


def body(query_rows, key_rows, value_rows, out_grad, out_weight, neighbours, counts):
    row_count, col_count = query_rows.shape
    blocks = row_count // BS
    slots = neighbours.shape[1]
    pair_total = col_count // LANES
    groups = [1, 2, 1] if pair_total == 4 else [1] * pair_total
    starts = [sum(groups[:g]) for g in range(len(groups))]
    ctx_index = lax.axis_index("ctx")
    head_index = lax.axis_index("head")

    halos = []
    for start, pairs in zip(starts, groups):
        cols = slice(start * LANES, (start + pairs) * LANES)
        packed = jnp.concatenate([key_rows[:, cols], value_rows[:, cols]], axis=1)
        halos.append((shifted(packed, "ctx", 1), shifted(packed, "ctx", -1)))

    if lax.axis_size("head") == 2:
        other = lax.ppermute(out_grad, "head", [(0, 1), (1, 0)])
        first = jnp.where(head_index == 0, out_grad, other)
        second = jnp.where(head_index == 0, other, out_grad)
        cotangent = jnp.concatenate([first, second], axis=1)
    else:
        cotangent = lax.all_gather(out_grad, "head", axis=1, tiled=True)
    grad_attended = jnp.einsum(
        "ro,jo->rj", cotangent, out_weight, preferred_element_type=jnp.float32
    ).astype(jnp.bfloat16)

    first_block = ctx_index * blocks
    listed = lax.dynamic_slice_in_dim(neighbours, first_block, blocks, axis=0)
    active = lax.dynamic_slice_in_dim(counts, first_block, blocks, axis=0)
    places = jnp.clip(listed - (first_block - blocks), 0, 3 * blocks - 1)
    if slots % STEPS[0]:
        extra = STEPS[0] - slots % STEPS[0]
        places = jnp.concatenate([places] + [places[:, :1]] * extra, axis=1)
    places = places.reshape(-1)
    scale = (row_count * lax.axis_size("ctx")) ** (-0.5)

    query_parts, key_parts, value_parts, weight_parts = [], [], [], []
    for (left, right), start, pairs in zip(halos, starts, groups):
        width = pairs * LANES
        attended, dq, to_left, middle, to_right = group_attention(
            places,
            active,
            query_rows,
            grad_attended,
            key_rows,
            value_rows,
            left,
            right,
            start,
            pairs,
        )
        product = jnp.einsum("rj,ro->jo", attended, cotangent, preferred_element_type=jnp.float32)
        weight_parts.append(product)
        from_right = shifted(to_left, "ctx", -1).astype(jnp.float32)
        from_left = shifted(to_right, "ctx", 1).astype(jnp.float32)
        combined = (middle + from_right + from_left).astype(jnp.bfloat16)
        query_parts.append(dq)
        key_parts.append(combined[:, :width])
        value_parts.append(combined[:, width:])
    return (
        jnp.concatenate(query_parts, axis=1),
        jnp.concatenate(key_parts, axis=1),
        jnp.concatenate(value_parts, axis=1),
        summed_over_ctx(weight_parts) * scale,
    )


def solution(mesh):
    placed = (
        P("ctx", "head"),
        P("ctx", "head"),
        P("ctx", "head"),
        P("ctx", "head"),
        P("head", None),
        P(),
        P(),
    )
    return jax.shard_map(
        body,
        mesh=mesh,
        in_specs=placed,
        out_specs=(P("ctx", "head"), P("ctx", "head"), P("ctx", "head"), P("head", None)),
        check_vma=False,
    )
```

```python
import functools

import jax
import jax.numpy as jnp
from jax import lax
from jax.experimental import pallas as pl
from jax.experimental.pallas import tpu as pltpu
from jax.sharding import PartitionSpec as P

HD = 64
BS = 128
LANES = 2 * HD
STEPS = (4, 2)
FACTOR = HD ** (-0.5)

def mm(a, b):
    return jnp.dot(a, b, preferred_element_type=jnp.float32)


def shifted(x, axis, by):
    count = lax.axis_size(axis)
    pairs = [(i, i + by) for i in range(count) if 0 <= i + by < count]
    return lax.ppermute(x, axis, pairs)


def stacked(values, axis):
    at = lax.broadcasted_iota(jnp.int32, values.shape, axis)
    first = jnp.where(at < HD, values, 0.0)
    second = jnp.where(at >= HD, values, 0.0)
    return jnp.concatenate([first, second], axis=1 - axis).astype(jnp.bfloat16)


def own_parts(both):
    return jnp.concatenate([both[:HD, :BS], both[HD:, BS:]], axis=0)


def attention_kernel(
    places,
    active,
    *refs,
    blocks,
    slots,
    pairs,
):
    q_refs, g_refs, k_mids, v_mids = [refs[i * pairs : (i + 1) * pairs] for i in range(4)]
    (
        left_ref,
        right_ref,
        att_ref,
        dq_ref,
        out_left,
        out_mid,
        out_right,
        kw,
        vw,
        kt,
        vt,
        fixed,
        fixed_t,
        sc,
        peak,
        mass,
        acc,
        dk,
        dv,
    ) = refs[4 * pairs :]
    block = pl.program_id(0)
    width = pairs * LANES

    @pl.when(block == 0)
    def _():
        dk[...] = jnp.zeros_like(dk)
        dv[...] = jnp.zeros_like(dv)

        def place_block(b, carry):
            rows = pl.ds(pl.multiple_of(b * BS, BS), BS)
            for p in range(pairs):
                cols = slice(p * LANES, (p + 1) * LANES)
                vcols = slice(width + p * LANES, width + (p + 1) * LANES)
                for part, (kr, kc, vr, vc) in enumerate(
                    (
                        (left_ref, cols, left_ref, vcols),
                        (k_mids[p], slice(None), v_mids[p], slice(None)),
                        (right_ref, cols, right_ref, vcols),
                    )
                ):
                    at = part * blocks + b
                    kb = kr[rows, kc]
                    vb = vr[rows, vc]
                    kw[p, at] = kb
                    vw[p, at] = vb
                    kt[p, at] = kb.T
                    vt[p, at] = vb.T
            return carry

        lax.fori_loop(0, blocks, place_block, 0)

    count = active[block]
    large, small = STEPS
    full = (count + 1) // large
    rest = (jnp.maximum(count - full * large, 0) + small - 1) // small
    base = block * slots

    def sweep(visit):
        def large_trip(t, carry):
            visit(t * large, large)
            return carry

        def small_trip(t, carry):
            visit(full * large + t * small, small)
            return carry

        lax.fori_loop(0, full, large_trip, 0)
        lax.fori_loop(0, rest, small_trip, 0)

    q_cols, g_cols, gt = [], [], []
    for p in range(pairs):
        cols = slice(p * LANES, (p + 1) * LANES)
        q = q_refs[p][...].astype(jnp.float32)
        g = g_refs[p][...].astype(jnp.float32)
        gt.append(g.T)
        fixed[p, 0] = stacked(q, 1)
        fixed[p, 1] = stacked(g, 1)
        q_cols.append(stacked(q.T * FACTOR, 0))
        g_cols.append(stacked(gt[p], 0))
    for p in range(pairs):
        fixed_t[p, 0] = q_cols[p]
        fixed_t[p, 1] = g_cols[p]

    def slot_places(start, step):
        return [places[base + start + u] for u in range(step)]

    for p in range(pairs):
        peak[p] = jnp.full(peak.shape[1:], -1e30, jnp.float32)
        mass[p] = jnp.zeros(mass.shape[1:], jnp.float32)

    def score_step(start, step):
        at = slot_places(start, step)
        for p in range(pairs):
            both = mm(jnp.concatenate([kw[p, a] for a in at], axis=0), fixed_t[p, 0])
            for u in range(step):
                slot = start + u
                rows = pl.ds(pl.multiple_of(slot * BS, BS), BS)
                s = both[u * BS : (u + 1) * BS]
                m = jnp.max(s, axis=0, keepdims=True)
                e = jnp.exp(s - m)
                sc[p, rows, :] = e
                peak[p, pl.ds(slot, 1), :] = jnp.where(slot < count, m, -1e30)
                mass[p, pl.ds(slot, 1), :] = jnp.sum(e, axis=0, keepdims=True)

    sweep(score_step)
    for p in range(pairs):
        ratio = jnp.exp(peak[p] - jnp.max(peak[p], axis=0, keepdims=True))
        total = jnp.sum(mass[p] * ratio, axis=0, keepdims=True)
        peak[p] = ratio * (1.0 / total)

    def weights(p, slot):
        rows = pl.ds(pl.multiple_of(slot * BS, BS), BS)
        return sc[p, rows, :] * peak[p, pl.ds(slot, 1), :]

    def sum_step(start, step):
        at = slot_places(start, step)
        for p in range(pairs):
            w = jnp.concatenate(
                [weights(p, start + u).astype(jnp.bfloat16) for u in range(step)], axis=0
            )
            v_t = jnp.concatenate([vt[p, a] for a in at], axis=1)
            acc[p] += mm(v_t, w)

    acc[...] = jnp.zeros_like(acc)
    sweep(sum_step)
    dots = []
    for p in range(pairs):
        cols = slice(p * LANES, (p + 1) * LANES)
        o_t = own_parts(acc[p]).astype(jnp.bfloat16).astype(jnp.float32)
        att_ref[:, cols] = o_t.T.astype(jnp.bfloat16)
        prod = o_t * gt[p]
        dots.append(
            jnp.concatenate(
                [
                    jnp.sum(prod[:HD], axis=0, keepdims=True),
                    jnp.sum(prod[HD:], axis=0, keepdims=True),
                ],
                axis=1,
            )
        )

    def grad_step(start, step):
        at = slot_places(start, step)
        for p in range(pairs):
            dp = mm(jnp.concatenate([vw[p, a] for a in at], axis=0), fixed_t[p, 1])
            w = [weights(p, start + u) for u in range(step)]
            ds = [w[u] * (dp[u * BS : (u + 1) * BS] - dots[p]) for u in range(step)]
            w = jnp.concatenate(w, axis=0).astype(jnp.bfloat16)
            ds = jnp.concatenate(ds, axis=0).astype(jnp.bfloat16)
            grad_v = mm(w, fixed[p, 1])
            grad_k = mm(ds, fixed[p, 0])
            k_t = jnp.concatenate([kt[p, a] for a in at], axis=1)
            acc[p] += mm(k_t, ds)
            for u in range(step):
                dv[p, at[u]] += grad_v[u * BS : (u + 1) * BS]
                dk[p, at[u]] += grad_k[u * BS : (u + 1) * BS]

    acc[...] = jnp.zeros_like(acc)
    sweep(grad_step)
    for p in range(pairs):
        cols = slice(p * LANES, (p + 1) * LANES)
        dq_ref[:, cols] = (own_parts(acc[p]).T * FACTOR).astype(jnp.bfloat16)

    @pl.when(block == blocks - 1)
    def _():
        def put_block(b, carry):
            rows = pl.ds(pl.multiple_of(b * BS, BS), BS)
            for p in range(pairs):
                cols = slice(p * LANES, (p + 1) * LANES)
                vcols = slice(width + p * LANES, width + (p + 1) * LANES)
                for part, out in enumerate((out_left, out_mid, out_right)):
                    at = part * blocks + b
                    out[rows, cols] = (dk[p, at] * FACTOR).astype(out.dtype)
                    out[rows, vcols] = dv[p, at].astype(out.dtype)
            return carry

        lax.fori_loop(0, blocks, put_block, 0)


def group_attention(places, active, queries, grads, keys, values, left, right, start, pairs):
    rows = queries.shape[0]
    blocks = rows // BS
    slots = places.shape[0] // blocks
    width = pairs * LANES
    tiles = [pl.BlockSpec((BS, LANES), lambda i, *_, at=start + p: (i, at)) for p in range(pairs)]
    wholes = [pl.BlockSpec((rows, LANES), lambda i, *_, at=start + p: (0, at)) for p in range(pairs)]
    out_tile = pl.BlockSpec((BS, width), lambda i, *_: (i, 0))
    packed = pl.BlockSpec((rows, 2 * width), lambda i, *_: (0, 0))
    window = (pairs, 3 * blocks, BS, LANES)
    padded = slots
    return pl.pallas_call(
        functools.partial(attention_kernel, blocks=blocks, slots=slots, pairs=pairs),
        grid_spec=pltpu.PrefetchScalarGridSpec(
            num_scalar_prefetch=2,
            grid=(blocks,),
            in_specs=[*tiles, *tiles, *wholes, *wholes, packed, packed],
            out_specs=[out_tile, out_tile, packed, packed, packed],
            scratch_shapes=[
                pltpu.VMEM(window, jnp.bfloat16),
                pltpu.VMEM(window, jnp.bfloat16),
                pltpu.VMEM(window, jnp.bfloat16),
                pltpu.VMEM(window, jnp.bfloat16),
                pltpu.VMEM((pairs, 2, 2 * BS, LANES), jnp.bfloat16),
                pltpu.VMEM((pairs, 2, LANES, 2 * BS), jnp.bfloat16),
                pltpu.VMEM((pairs, padded * BS, 2 * BS), jnp.float32),
                pltpu.VMEM((pairs, (padded + 7) // 8 * 8, 2 * BS), jnp.float32),
                pltpu.VMEM((pairs, (padded + 7) // 8 * 8, 2 * BS), jnp.float32),
                pltpu.VMEM((pairs, LANES, 2 * BS), jnp.float32),
                pltpu.VMEM(window, jnp.float32),
                pltpu.VMEM(window, jnp.float32),
            ],
        ),
        out_shape=[
            jax.ShapeDtypeStruct((rows, width), jnp.bfloat16),
            jax.ShapeDtypeStruct((rows, width), jnp.bfloat16),
            jax.ShapeDtypeStruct((rows, 2 * width), jnp.bfloat16),
            jax.ShapeDtypeStruct((rows, 2 * width), jnp.float32),
            jax.ShapeDtypeStruct((rows, 2 * width), jnp.bfloat16),
        ],
        compiler_params=pltpu.CompilerParams(
            dimension_semantics=("arbitrary",), vmem_limit_bytes=48 * 1024 * 1024
        ),
        cost_estimate=pl.CostEstimate(
            flops=7 * 2 * 2 * blocks * slots * pairs * BS * BS * LANES,
            bytes_accessed=rows * width * 32,
            transcendentals=2 * blocks * slots * pairs * BS * BS,
        ),
    )(
        places,
        active,
        *[queries] * pairs,
        *[grads] * pairs,
        *[keys] * pairs,
        *[values] * pairs,
        left,
        right,
    )


def sum_kernel(*refs, sizes, count):
    parts, (full, acc, send, *landing, send_sems, recv_sems) = refs[:count], refs[count:]
    me = lax.axis_index("ctx")
    stages = []
    stride = 1
    for size in sizes:
        stages.append((size, stride, lax.rem(me // stride, size)))
        stride *= size

    def peer(stage, away):
        size, stride, mine = stage
        other = lax.rem(mine + away, size)
        return other, me + (other - mine) * stride

    barrier = pltpu.get_barrier_semaphore()
    greeted = 0
    for stage in stages:
        for away in range(1, stage[0]):
            pl.semaphore_signal(
                barrier,
                inc=1,
                device_id={"ctx": peer(stage, away)[1]},
                device_id_type=pl.DeviceIdType.MESH,
            )
            greeted += 1
    at = 0
    for part in parts:
        acc[pl.ds(at, part.shape[0]), :] = part[...]
        at += part.shape[0]
    pl.semaphore_wait(barrier, greeted)

    def copy(src, dst, sem, device):
        return pltpu.make_async_remote_copy(
            src_ref=src,
            dst_ref=dst,
            send_sem=send_sems.at[sem],
            recv_sem=recv_sems.at[sem],
            device_id={"ctx": device},
            device_id_type=pl.DeviceIdType.MESH,
        )

    rows = acc.shape[0]
    start = 0
    sem = 0
    pending = []
    spans = []
    for stage, land in zip(stages, landing):
        size, _, mine = stage
        spans.append((start, rows))
        piece = rows // size
        copies = []
        for away in range(1, size):
            other, device = peer(stage, away)
            span = pl.ds(pl.multiple_of(start + other * piece, 16), piece)
            send[span, :] = acc[span, :].astype(jnp.bfloat16)
            one = copy(send.at[span, :], land.at[away - 1], sem, device)
            one.start()
            copies.append(one)
            sem += 1
        start = start + mine * piece
        own = pl.ds(pl.multiple_of(start, 16), piece)
        for one in copies:
            one.wait_recv()
        total = acc[own, :]
        for away in range(1, size):
            total = total + land[away - 1].astype(jnp.float32)
        acc[own, :] = total
        rows = piece
        pending += copies
    own = pl.ds(pl.multiple_of(start, 16), rows)
    full[own, :] = acc[own, :].astype(jnp.bfloat16)
    for stage, (outer, outer_rows) in zip(stages[::-1], spans[::-1]):
        size, _, mine = stage
        piece = outer_rows // size
        span = pl.ds(pl.multiple_of(outer + mine * piece, 16), piece)
        copies = []
        for away in range(1, size):
            one = copy(full.at[span, :], full.at[span, :], sem, peer(stage, away)[1])
            one.start()
            copies.append(one)
            sem += 1
        for one in copies:
            one.wait_recv()
        pending += copies
    for one in pending:
        one.wait_send()


def summed_over_ctx(parts):
    count = lax.axis_size("ctx")
    rows = sum(part.shape[0] for part in parts)
    cols = parts[0].shape[1]
    rest = count // 2
    inner = 2 if rest <= 8 else 8
    sizes = (2, inner, rest // inner)
    if rows % (16 * count) or 2 * inner * sizes[2] != count:
        return lax.psum(jnp.concatenate(parts, axis=0), "ctx")
    landing = []
    left = rows
    for size in sizes:
        left //= size
        landing.append(pltpu.VMEM((size - 1, left, cols), jnp.bfloat16))
    copies = 2 * sum(size - 1 for size in sizes)
    out = pl.pallas_call(
        functools.partial(sum_kernel, sizes=sizes, count=len(parts)),
        out_shape=jax.ShapeDtypeStruct((rows, cols), jnp.bfloat16),
        in_specs=[pl.BlockSpec(memory_space=pltpu.VMEM)] * len(parts),
        out_specs=pl.BlockSpec(memory_space=pltpu.VMEM),
        scratch_shapes=[
            pltpu.VMEM((rows, cols), jnp.float32),
            pltpu.VMEM((rows, cols), jnp.bfloat16),
            *landing,
            pltpu.SemaphoreType.DMA((copies,)),
            pltpu.SemaphoreType.DMA((copies,)),
        ],
        compiler_params=pltpu.CompilerParams(
            collective_id=0, has_side_effects=True, vmem_limit_bytes=32 * 1024 * 1024
        ),
        cost_estimate=pl.CostEstimate(
            flops=rows * cols * 4, bytes_accessed=rows * cols * 40, transcendentals=0
        ),
    )(*parts)
    return out.astype(jnp.float32)


def body(query_rows, key_rows, value_rows, out_grad, out_weight, neighbours, counts):
    row_count, col_count = query_rows.shape
    blocks = row_count // BS
    slots = neighbours.shape[1]
    pair_total = col_count // LANES
    groups = [2] * (pair_total // 2) + [1] * (pair_total % 2)
    starts = [sum(groups[:g]) for g in range(len(groups))]
    ctx_index = lax.axis_index("ctx")
    head_index = lax.axis_index("head")

    halos = []
    for start, pairs in zip(starts, groups):
        cols = slice(start * LANES, (start + pairs) * LANES)
        packed = jnp.concatenate([key_rows[:, cols], value_rows[:, cols]], axis=1)
        halos.append((shifted(packed, "ctx", 1), shifted(packed, "ctx", -1)))

    if lax.axis_size("head") == 2:
        other = lax.ppermute(out_grad, "head", [(0, 1), (1, 0)])
        first = jnp.where(head_index == 0, out_grad, other)
        second = jnp.where(head_index == 0, other, out_grad)
        cotangent = jnp.concatenate([first, second], axis=1)
    else:
        cotangent = lax.all_gather(out_grad, "head", axis=1, tiled=True)
    grad_attended = jnp.einsum(
        "ro,jo->rj", cotangent, out_weight, preferred_element_type=jnp.float32
    ).astype(jnp.bfloat16)

    first_block = ctx_index * blocks
    listed = lax.dynamic_slice_in_dim(neighbours, first_block, blocks, axis=0)
    active = lax.dynamic_slice_in_dim(counts, first_block, blocks, axis=0)
    places = jnp.clip(listed - (first_block - blocks), 0, 3 * blocks - 1)
    if slots % STEPS[0]:
        extra = STEPS[0] - slots % STEPS[0]
        places = jnp.concatenate([places] + [places[:, :1]] * extra, axis=1)
    places = places.reshape(-1)
    scale = (row_count * lax.axis_size("ctx")) ** (-0.5)

    query_parts, key_parts, value_parts, weight_parts = [], [], [], []
    for (left, right), start, pairs in zip(halos, starts, groups):
        width = pairs * LANES
        attended, dq, to_left, middle, to_right = group_attention(
            places,
            active,
            query_rows,
            grad_attended,
            key_rows,
            value_rows,
            left,
            right,
            start,
            pairs,
        )
        product = jnp.einsum("rj,ro->jo", attended, cotangent, preferred_element_type=jnp.float32)
        weight_parts.append(product)
        from_right = shifted(to_left, "ctx", -1).astype(jnp.float32)
        from_left = shifted(to_right, "ctx", 1).astype(jnp.float32)
        combined = (middle + from_right + from_left).astype(jnp.bfloat16)
        query_parts.append(dq)
        key_parts.append(combined[:, :width])
        value_parts.append(combined[:, width:])
    return (
        jnp.concatenate(query_parts, axis=1),
        jnp.concatenate(key_parts, axis=1),
        jnp.concatenate(value_parts, axis=1),
        summed_over_ctx(weight_parts) * scale,
    )


def solution(mesh):
    placed = (
        P("ctx", "head"),
        P("ctx", "head"),
        P("ctx", "head"),
        P("ctx", "head"),
        P("head", None),
        P(),
        P(),
    )
    return jax.shard_map(
        body,
        mesh=mesh,
        in_specs=placed,
        out_specs=(P("ctx", "head"), P("ctx", "head"), P("ctx", "head"), P("head", None)),
        check_vma=False,
    )
```
